512 devices in a mesh: leaf: 32 (over x, y, core), front: 16 (over z).
Axes of the slice: x: 4, y: 4, z: 16, core: 2. Of those that a mesh axis runs over, the one named last changes fastest.
Arguments:
- panel_0: float32 [2, 1024, 1024], P(None, 'front', 'leaf'), as said below
- panel_1: float32 [2, 1024, 2048], P(None, 'front', 'leaf'), as said below
- panel_2: float32 [2, 1024, 4096], P(None, 'front', 'leaf'), as said below
- panel_3: float32 [2, 1024, 8192], P(None, 'front', 'leaf'), as said below
- load_0: float32 [1024, 128], P('leaf'), may hold values from -6 to 6
- load_1: float32 [2048, 128], P('leaf'), may hold values from -6 to 6
- load_2: float32 [4096, 128], P('leaf'), may hold values from -6 to 6
- load_3: float32 [8192, 128], P('leaf'), may hold values from -6 to 6
- inflow: float32 [8, 1024, 128], P(None, 'front'), may hold values from -6 to 6
- above_solution: float32 [1024, 128], replicated, may hold values from -6 to 6
- block_maps: int32 [14, 16], replicated, may hold values from 0 to 31, as said below
Outputs:
- solution_0: float32 [1024, 128], P(('leaf', 'front'))
- solution_1: float32 [2048, 128], P(('leaf', 'front'))
- solution_2: float32 [4096, 128], P(('leaf', 'front'))
- solution_3: float32 [8192, 128], P(('leaf', 'front'))
- top_update: float32 [1024, 128], P('front')
The draws below stay inside these ranges and needn't reach their ends.
Inputs may be any that keep to these rules, and one draw needn't show every extreme that they name: `block_maps`: the 16 entries of each row are distinct. `panel_0`: within each front the pivot block K is lower triangular with diagonal entries of 0.8 to 1.25. `panel_1`: within each front the pivot block K is lower triangular with diagonal entries of 0.8 to 1.25. `panel_2`: within each front the pivot block K is lower triangular with diagonal entries of 0.8 to 1.25. `panel_3`: within each front the pivot block K is lower triangular with diagonal entries of 0.8 to 1.25.
All inputs are finite; a program needn't handle non-finite values.
Results may differ from the reference program's by a relative error of at most 0.00013.
Values sent between devices are 32-bit elements; how exact they have to be, the bound alone decides.
No kernel may reach another device: no remote copies, remote signals or barrier semaphores. Data moves between devices by JAX's collectives and lax.ppermute only.
A program may use at most 64 MiB of HBM per device.

```python
import math
import jax
import jax.numpy as jnp
from jax import lax

SB = 64
RHS_COUNT = 128
LEVELS = 4
NB = 16
SEPARATOR_ROWS = 1024


def panel_draw(key, level_id):
    col_count = 2 ** level_id * SEPARATOR_ROWS
    key_lower, key_couple, key_diag = jax.random.split(key, 3)
    lower_draw = jax.random.normal(key_lower, (SEPARATOR_ROWS, col_count), jnp.float32)
    couple_draw = jax.random.normal(key_couple, (SEPARATOR_ROWS, col_count), jnp.float32)
    diagonal = jax.random.uniform(key_diag, (SEPARATOR_ROWS, col_count), jnp.float32, 0.8, 1.25)
    row_index = lax.broadcasted_iota(jnp.int32, (SEPARATOR_ROWS, col_count), 0)
    col_index = lax.broadcasted_iota(jnp.int32, (SEPARATOR_ROWS, col_count), 1) % SEPARATOR_ROWS
    pivot_block = jnp.where(col_index < row_index, 0.6 / math.sqrt(SEPARATOR_ROWS) * lower_draw, 0.0)
    pivot_block = pivot_block + jnp.where(col_index == row_index, diagonal, 0.0)
    coupling = 0.5 / math.sqrt(SEPARATOR_ROWS) * couple_draw
    return jnp.stack([pivot_block, coupling]).astype(jnp.float32)


def draw_panel_0(key, part):
    return panel_draw(jax.random.fold_in(key, 11), 0)


def draw_panel_1(key, part):
    return panel_draw(jax.random.fold_in(key, 12), 1)


def draw_panel_2(key, part):
    return panel_draw(jax.random.fold_in(key, 13), 2)


def draw_panel_3(key, part):
    return panel_draw(jax.random.fold_in(key, 14), 3)


def one_row(row_key):
    return jax.random.permutation(row_key, 2 * NB)


def draw_block_maps(key, part):
    row_count = 2 ** LEVELS - 2
    row_keys = jax.random.split(jax.random.fold_in(key, 7), row_count)
    permuted = jax.vmap(one_row)(row_keys).astype(jnp.int32)
    top_pos = jnp.argmax(permuted[0] == 2 * NB - 1)
    low_pos = jnp.argmax(permuted[1] == 0)
    permuted = permuted.at[0].set(jnp.roll(permuted[0], -top_pos))
    permuted = permuted.at[1].set(jnp.roll(permuted[1], -low_pos))
    return permuted[:, :NB].astype(jnp.int32)


def block_scale(key, shape, cuts, smallest, top_value):
    def one(position, parts):
        heights = jax.random.uniform(jax.random.fold_in(jax.random.fold_in(key, 6), position), (parts,), jnp.float32, smallest / len(cuts), top_value / len(cuts))
        return jnp.repeat(jnp.exp(heights), shape[position] // parts).reshape((-1,) + (1,) * (len(shape) - position - 1))

    factor_of = one(*cuts[0])
    for cut in cuts[1:]:
        factor_of = factor_of * one(*cut)
    return factor_of


def normal_values(key, extent, scale, most, shards=(), held_as=jnp.bfloat16):
    factor_of = block_scale(key, extent, shards, -0.22, 0.18) if shards else 1.0
    array = jax.random.normal(key, extent, jnp.float32) * scale * factor_of
    return jnp.minimum(jnp.maximum(array, -most), most).astype(held_as)


def setup_inputs(seed: int = 0) -> dict:
    streams_of = jax.random.split(jax.random.key(seed), 12)
    panel_0 = draw_panel_0(jax.random.fold_in(streams_of[11], 71), 0)
    panel_1 = draw_panel_1(jax.random.fold_in(streams_of[11], 71), 0)
    panel_2 = draw_panel_2(jax.random.fold_in(streams_of[11], 71), 0)
    panel_3 = draw_panel_3(jax.random.fold_in(streams_of[11], 71), 0)
    load_0 = normal_values(streams_of[4], (SEPARATOR_ROWS, RHS_COUNT), 1.0, 6.0, ((0, 32),), jnp.float32)
    load_1 = normal_values(streams_of[5], (2 * SEPARATOR_ROWS, RHS_COUNT), 1.0, 6.0, ((0, 32),), jnp.float32)
    load_2 = normal_values(streams_of[6], (4 * SEPARATOR_ROWS, RHS_COUNT), 1.0, 6.0, ((0, 32),), jnp.float32)
    load_3 = normal_values(streams_of[7], (8 * SEPARATOR_ROWS, RHS_COUNT), 1.0, 6.0, ((0, 32),), jnp.float32)
    inflow = normal_values(streams_of[8], (8, SEPARATOR_ROWS, RHS_COUNT), 1.0, 6.0, ((1, 16),), jnp.float32)
    above_solution = normal_values(streams_of[9], (SEPARATOR_ROWS, RHS_COUNT), 1.0, 6.0, (), jnp.float32)
    block_maps = draw_block_maps(jax.random.fold_in(streams_of[11], 71), 0)
    return {"panel_0": panel_0, "panel_1": panel_1, "panel_2": panel_2, "panel_3": panel_3, "load_0": load_0, "load_1": load_1, "load_2": load_2, "load_3": load_3, "inflow": inflow, "above_solution": above_solution, "block_maps": block_maps}


exact_precision = lax.Precision.HIGHEST


def product(left, right):
    return jnp.dot(left, right, precision=exact_precision, preferred_element_type=jnp.float32)


def place_blocks(map_row, values):
    targets = jnp.arange(2 * NB, dtype=jnp.int32)
    selector_matrix = (targets[:, None] == map_row[None, :].astype(jnp.int32)).astype(jnp.float32)
    factor_blocks = values.reshape(NB, SB, RHS_COUNT)
    return jnp.einsum("du,uye->dye", selector_matrix, factor_blocks, precision=exact_precision).reshape(2 * SEPARATOR_ROWS, RHS_COUNT)


def take_blocks(map_row, stacked):
    targets = jnp.arange(2 * NB, dtype=jnp.int32)
    selector_matrix = (map_row[:, None].astype(jnp.int32) == targets[None, :]).astype(jnp.float32)
    factor_blocks = stacked.reshape(2 * NB, SB, RHS_COUNT)
    return jnp.einsum("gq,qzk->gzk", selector_matrix, factor_blocks, precision=exact_precision).reshape(SEPARATOR_ROWS, RHS_COUNT)


def reference(panel_0, panel_1, panel_2, panel_3, load_0, load_1, load_2, load_3, inflow, above_solution, block_maps):
    panels = (panel_0, panel_1, panel_2, panel_3)
    load_list = (load_0, load_1, load_2, load_3)
    solved = [None] * LEVELS
    child_updates = None
    for level_id in range(LEVELS - 1, -1, -1):
        level_solved = []
        level_updates = []
        for front_id in range(2 ** level_id):
            inverse_block = panels[level_id][0, :, front_id * SEPARATOR_ROWS:(front_id + 1) * SEPARATOR_ROWS]
            coupling = panels[level_id][1, :, front_id * SEPARATOR_ROWS:(front_id + 1) * SEPARATOR_ROWS]
            right_side = load_list[level_id][front_id * SEPARATOR_ROWS:(front_id + 1) * SEPARATOR_ROWS]
            if level_id == LEVELS - 1:
                border = inflow[front_id]
            else:
                base_row = 2 ** (level_id + 1) - 2 + 2 * front_id
                gathered = place_blocks(block_maps[base_row], child_updates[2 * front_id])
                gathered = gathered + place_blocks(block_maps[base_row + 1], child_updates[2 * front_id + 1])
                right_side = right_side + gathered[:SEPARATOR_ROWS]
                border = gathered[SEPARATOR_ROWS:]
            level_solved.append(product(inverse_block, right_side))
            level_updates.append(border - product(coupling, right_side))
        solved[level_id] = level_solved
        child_updates = level_updates
    top_update = child_updates[0]
    uppers = [above_solution]
    outputs = []
    for level_id in range(LEVELS):
        results = []
        for front_id in range(2 ** level_id):
            inverse_block = panels[level_id][0, :, front_id * SEPARATOR_ROWS:(front_id + 1) * SEPARATOR_ROWS]
            coupling = panels[level_id][1, :, front_id * SEPARATOR_ROWS:(front_id + 1) * SEPARATOR_ROWS]
            result = product(inverse_block.T, solved[level_id][front_id]) - product(coupling.T, uppers[front_id])
            results.append(result)
        outputs.append(jnp.concatenate(results, 0))
        if level_id < LEVELS - 1:
            next_uppers = []
            for child_id in range(2 ** (level_id + 1)):
                parent = child_id // 2
                stacked = jnp.concatenate([results[parent], uppers[parent]], 0)
                next_uppers.append(take_blocks(block_maps[2 ** (level_id + 1) - 2 + child_id], stacked))
            uppers = next_uppers
    return outputs[0], outputs[1], outputs[2], outputs[3], top_update
```

```python
import jax
import jax.numpy as jnp
from jax import lax
from jax.sharding import Mesh, PartitionSpec as P

exact = lax.Precision.HIGHEST
LEAF = ("xh", "xl", "y", "c")
SWAP = [(0, 1), (1, 0)]


def dot_nt(left, right):
    return lax.dot_general(left, right, (((1,), (1,)), ((), ())), precision=exact)


def dot_nn(left, right):
    return lax.dot_general(left, right, (((1,), (0,)), ((), ())), precision=exact)


def exchange(value, axes):
    return lax.all_to_all(value, axes, 0, 0)


def to_all(value, count):
    return jnp.broadcast_to(value[None], (count,) + value.shape)


def on_device(
    panel_0,
    panel_1,
    panel_2,
    panel_3,
    load_0,
    load_1,
    load_2,
    load_3,
    inflow,
    above_solution,
    block_maps,
):
    xh, xl = lax.axis_index("xh"), lax.axis_index("xl")
    y, c, z = lax.axis_index("y"), lax.axis_index("c"), lax.axis_index("z")
    x = 2 * xh + xl
    y_low = y & 1
    front_3 = 2 * x + (y >> 1)

    own_rows = jnp.concatenate(
        [panel_3[0], panel_3[1], panel_2[0], panel_1[0], panel_0[0], panel_0[1]], 1
    )
    gathered = lax.all_gather(own_rows, "z", axis=0, tiled=True)

    def pick_columns(value):
        return lax.dynamic_slice_in_dim(value, z * 8 + c * 4, 4, 1).T

    def pick_both(value):
        mine = lax.dynamic_slice_in_dim(value, z * 8, 8, 1).T
        return mine.reshape(2, 4, -1)

    loads = jnp.concatenate([pick_both(load_0), pick_both(load_1), pick_both(load_2)], 2)
    loads = exchange(loads, "c")
    load_0c = loads[:, :, :32].transpose(1, 0, 2).reshape(4, 64)
    load_1c = loads[:, :, 32:96].transpose(1, 0, 2).reshape(4, 128)
    load_2c = loads[:, :, 96:].transpose(1, 0, 2).reshape(4, 256)
    above = pick_columns(above_solution)

    part_3 = jnp.einsum("ksc,cr->rks", panel_3, load_3, precision=exact)
    border_3 = lax.dynamic_index_in_dim(inflow, front_3, 0, keepdims=False).T
    first = (y_low + c == 0).astype(jnp.float32)
    part_3 = jnp.concatenate([part_3[:, 0], first * border_3 - part_3[:, 1]], 1)
    couple = jnp.concatenate(
        [panel_2[1], jnp.concatenate([panel_1[1, :32], panel_1[1, 32:]], 1)], 0
    )
    payload = jnp.concatenate([part_3.reshape(16, 8, 128), to_all(couple, 16)], 1)
    got = exchange(payload, "z")
    vec = got[:, :8].reshape(16, 8, 2, 64).transpose(2, 1, 0, 3).reshape(2, 8, 1024)
    couple_2 = got[:, 8:72].reshape(1024, 128)
    couple_1 = got[:, 72:]
    couple_1 = jnp.stack([couple_1[..., :64], couple_1[..., 64:]], 1).reshape(1024, 64)

    couple_2o = lax.ppermute(couple_2, "c", SWAP)
    couple_1o = lax.ppermute(couple_1, "c", SWAP)

    def by_core(own, other):
        return jnp.where(c == 0, own, other), jnp.where(c == 0, other, own)

    def chip_nt(vector, own, other):
        width = own.shape[1]
        low, high = vector[:, :width], vector[:, width:]
        mine, rest = jnp.where(c == 0, low, high), jnp.where(c == 0, high, low)
        return dot_nt(mine, own) + dot_nt(rest, other)

    def chip_columns(keep, keep_o, take, take_o, y_vec, s_vec):
        own = dot_nn(y_vec, keep) - dot_nn(s_vec, take)
        other = dot_nn(y_vec, keep_o) - dot_nn(s_vec, take_o)
        low, high = by_core(own, other)
        return jnp.concatenate([low, high], 1)

    u_send = vec[1].reshape(2, 4, 1024)
    u_send = jnp.broadcast_to(u_send[None], (4, 2, 4, 1024))
    y_send = vec[0].reshape(2, 4, 2, 512).transpose(2, 0, 1, 3)
    y_send = jnp.broadcast_to(y_send[None], (2, 2, 2, 4, 512)).reshape(4, 2, 4, 512)
    got = exchange(jnp.concatenate([u_send, y_send], 3).reshape(8, 4, 1536), ("y", "c"))
    got = got.reshape(2, 4, 4, 1536).sum(1)
    update = got[..., :1024]
    y3_piece = lax.dynamic_index_in_dim(got[..., 1024:], y >> 1, 0, keepdims=False)

    def lifted(update, base, block, count):
        maps = lax.dynamic_slice_in_dim(block_maps, base, 2, 0).reshape(32)
        targets = block * count + jnp.arange(count, dtype=jnp.int32)
        targets = jnp.concatenate([targets, targets + 16])
        chosen = (maps[:, None] == targets[None, :]).astype(jnp.float32)
        blocks = update.reshape(2, 4, 16, 64).transpose(1, 0, 2, 3).reshape(4, 32, 64)
        placed = jnp.einsum("rnk,np->rpk", blocks, chosen, precision=exact)
        separator = placed[:, :count].reshape(4, count * 64)
        border = placed[:, count:].reshape(4, count * 64)
        whole = jnp.zeros((4, 1024), jnp.float32)
        border = lax.dynamic_update_slice_in_dim(whole, border, block * count * 64, 1)
        return separator, border

    separator, border = lifted(update, 6 + 2 * x, y, 4)
    b_2 = separator + load_2c
    update = border - chip_nt(b_2, couple_2, couple_2o)
    update = exchange(to_all(update, 8), ("xl", "y")).reshape(2, 4, 4, 1024).sum(1)

    separator, border = lifted(update, 2 + 2 * xh, 4 * xl + y, 2)
    b_1 = separator + load_1c
    update = border - chip_nt(b_1, couple_1, couple_1o)
    update = exchange(to_all(update, 16), ("xh", "xl", "y")).reshape(2, 8, 4, 1024).sum(1)

    top, rest = gathered[:, 640:], gathered[:, :640]
    top_o = lax.ppermute(top, "c", SWAP)
    rest_o = lax.ppermute(rest, "c", SWAP)
    pivot_1, pivot_1o = top[:, :64], top_o[:, :64]
    pivot_0, pivot_0o = top[:, 64:96], top_o[:, 64:96]
    couple_0, couple_0o = top[:, 96:], top_o[:, 96:]
    pivot_3, pivot_3o = rest[:, :256], rest_o[:, :256]
    couple_3, couple_3o = rest[:, 256:512], rest_o[:, 256:512]
    pivot_2, pivot_2o = rest[:, 512:], rest_o[:, 512:]
    separator, border = lifted(update, 0, 4 * x + y, 1)
    b_0 = separator + load_0c
    y0_part = chip_nt(b_0, pivot_0, pivot_0o)
    u0_part = border - chip_nt(b_0, couple_0, couple_0o)
    y1_part = chip_nt(b_1, pivot_1, pivot_1o)
    u0_send = u0_part.reshape(4, 16, 64).transpose(1, 0, 2)
    y1_send = y1_part.reshape(4, 8, 128).transpose(1, 0, 2)
    y1_send = jnp.concatenate([y1_send, y1_send], 0)
    payload = jnp.concatenate([to_all(y0_part, 16), y1_send, u0_send], 2)
    got = exchange(payload, ("xh", "xl", "y"))
    y_0 = got[..., :1024].sum(0)
    u0_piece = got[..., 1152:].sum(0)
    y1_piece = got[..., 1024:1152].reshape(2, 8, 4, 128).sum(1)
    y1_piece = lax.dynamic_index_in_dim(y1_piece, xh, 0, keepdims=False)

    def taken(row, x_vec, s_vec):
        chosen_map = lax.dynamic_index_in_dim(block_maps, row, 0, keepdims=False)
        targets = jnp.arange(32, dtype=jnp.int32)
        chosen = (targets[:, None] == chosen_map[None, :]).astype(jnp.float32)
        stacked = jnp.concatenate([x_vec, s_vec], 1).reshape(4, 32, 64)
        return jnp.einsum("rqk,qn->rnk", stacked, chosen, precision=exact).reshape(4, 1024)

    x0_piece = chip_columns(pivot_0, pivot_0o, couple_0, couple_0o, y_0, above)
    y2_part = chip_nt(b_2, pivot_2, pivot_2o)
    y2_send = y2_part.reshape(4, 4, 256).transpose(1, 0, 2)
    y2_send = to_all(y2_send, 4).reshape(16, 4, 256)
    same = jnp.concatenate([x0_piece, u0_piece, y1_piece], 1)
    payload = jnp.concatenate([to_all(same, 16), y2_send], 2)
    got = exchange(payload, ("xh", "xl", "y"))
    x_0 = got[..., :64].transpose(1, 0, 2).reshape(4, 1024)
    u_0 = got[..., 64:128].transpose(1, 0, 2).reshape(4, 1024)
    y_1 = got[..., 128:256].reshape(2, 8, 4, 128)
    y_1 = lax.dynamic_index_in_dim(y_1, xh, 0, keepdims=False)
    y_1 = y_1.transpose(1, 0, 2).reshape(4, 1024)
    y2_piece = lax.dynamic_index_in_dim(
        got[..., 256:].reshape(4, 4, 4, 256).sum(1), x, 0, keepdims=False
    )

    s_1 = taken(xh, x_0, above)
    x1_piece = chip_columns(pivot_1, pivot_1o, couple_1, couple_1o, y_1, s_1)
    got = exchange(to_all(jnp.concatenate([x1_piece, y2_piece], 1), 8), ("xl", "y"))
    x_1 = got[..., :128].transpose(1, 0, 2).reshape(4, 1024)
    y_2 = lax.dynamic_index_in_dim(got[..., 128:].reshape(2, 4, 4, 256), xl, 0, keepdims=False)
    y_2 = y_2.transpose(1, 0, 2).reshape(4, 1024)

    s_2 = taken(2 + x, x_1, s_1)
    x2_piece = chip_columns(pivot_2, pivot_2o, couple_2, couple_2o, y_2, s_2)
    got = exchange(to_all(jnp.concatenate([x2_piece, y3_piece], 1), 4), "y")
    x_2 = got[..., :256].transpose(1, 0, 2).reshape(4, 1024)
    y_3 = lax.dynamic_index_in_dim(got[..., 256:].reshape(2, 2, 4, 512), y >> 1, 0, keepdims=False)
    y_3 = y_3.transpose(1, 0, 2).reshape(4, 1024)

    s_3 = taken(6 + front_3, x_2, s_2)
    x3_piece = chip_columns(pivot_3, pivot_3o, couple_3, couple_3o, y_3, s_3)

    def to_rows(piece):
        return piece.reshape(4, 2, 16, -1).transpose(1, 2, 0, 3)

    u0_rows = jnp.broadcast_to(u_0.reshape(4, 16, 64).transpose(1, 0, 2)[None], (2, 16, 4, 64))
    payload = jnp.concatenate(
        [
            to_rows(x3_piece),
            to_rows(x2_piece),
            to_rows(x1_piece),
            to_rows(x0_piece),
            jnp.zeros((2, 16, 4, 34), jnp.float32),
            u0_rows,
        ],
        3,
    )
    got = exchange(payload.reshape(32, 4, 128), ("c", "z"))
    got = got.reshape(2, 16, 4, 128).transpose(3, 1, 0, 2).reshape(128, 128)
    return (got[28:30], got[24:28], got[16:24], got[:16], got[64:])


def solution(mesh):
    fine = Mesh(mesh.devices.reshape(2, 2, 4, 2, 16), ("xh", "xl", "y", "c", "z"))
    panel = P(None, "z", LEAF)
    load = P(LEAF, None)
    in_specs = (panel,) * 4 + (load,) * 4 + (P(None, "z", None), P(), P())
    out_specs = (P(LEAF + ("z",), None),) * 4 + (P("z", None),)
    return jax.shard_map(
        on_device, mesh=fine, in_specs=in_specs, out_specs=out_specs, check_vma=False
    )
```

```python
import jax
import jax.numpy as jnp
from jax import lax
from jax.experimental import pallas as pl
from jax.experimental.pallas import tpu as pltpu
from jax.sharding import Mesh, PartitionSpec as P

exact = lax.Precision.HIGHEST
LEAF = ("xh", "xl", "y", "c")
SWAP = [(0, 1), (1, 0)]


def dot_nt(left, right):
    return lax.dot_general(left, right, (((1,), (1,)), ((), ())), precision=exact)


def dot_nn(left, right):
    return lax.dot_general(left, right, (((1,), (0,)), ((), ())), precision=exact)


def exchange(value, axes):
    return lax.all_to_all(value, axes, 0, 0)


def to_all(value, count):
    return jnp.broadcast_to(value[None], (count,) + value.shape)


def shape(*dims):
    return jax.ShapeDtypeStruct(dims, jnp.float32)


def pack_panels(p0_ref, p1_ref, p2_ref, p3_ref, out_ref):
    out_ref[:, :256] = p3_ref[0]
    out_ref[:, 256:512] = p3_ref[1]
    out_ref[:, 512:640] = p2_ref[0]
    out_ref[:, 640:768] = jnp.concatenate([p1_ref[0], p1_ref[1]], 1)
    blank = jnp.zeros((64, 64), jnp.float32)
    out_ref[:, 768:] = jnp.concatenate([p0_ref[0], p0_ref[1], blank], 1)


def first_parts(panel_ref, load_ref, inflow_ref, out_ref):
    x = 2 * lax.axis_index("xh") + lax.axis_index("xl")
    y, c = lax.axis_index("y"), lax.axis_index("c")
    keep = dot_nn(panel_ref[0], load_ref[...])
    take = dot_nn(panel_ref[1], load_ref[...])
    border = inflow_ref[2 * x + (y >> 1)]
    first = jnp.where((y & 1) + c == 0, 1.0, 0.0)
    both = jnp.concatenate([keep, first * border - take], 0)
    out_ref[...] = both.T.reshape(16, 8, 128)


def last_rows(got_ref, *out_refs):
    rows = got_ref[...].reshape(128, 128).T
    for ref, start in zip(out_refs, (28, 24, 16, 0, 64)):
        ref[...] = rows[start : start + ref.shape[0]]


def on_device(
    panel_0,
    panel_1,
    panel_2,
    panel_3,
    load_0,
    load_1,
    load_2,
    load_3,
    inflow,
    above_solution,
    block_maps,
):
    xh, xl = lax.axis_index("xh"), lax.axis_index("xl")
    y, c, z = lax.axis_index("y"), lax.axis_index("c"), lax.axis_index("z")
    x = 2 * xh + xl
    y_low = y & 1
    front_3 = 2 * x + (y >> 1)

    rows = pl.pallas_call(pack_panels, out_shape=shape(64, 896))(
        panel_0, panel_1, panel_2, panel_3
    )
    gathered = lax.all_gather(rows, "z", axis=0, tiled=True)
    rows, panel_3, load_3, inflow = lax.optimization_barrier((rows, panel_3, load_3, inflow))

    payload = pl.pallas_call(first_parts, out_shape=shape(16, 8, 128))(panel_3, load_3, inflow)
    payload, loads, above_in = lax.optimization_barrier(
        (payload, (load_0, load_1, load_2), above_solution)
    )
    got = exchange(payload, "z")

    loads = jnp.concatenate(loads, 0)
    loads = lax.dynamic_slice_in_dim(loads, z * 8, 8, 1).T
    loads_mine, loads_sent = jnp.where(c == 0, loads[:4], loads[4:]), jnp.where(c == 0, loads[4:], loads[:4])
    loads_other = lax.ppermute(loads_sent, "c", SWAP)

    def by_core(own, other):
        return jnp.where(c == 0, own, other), jnp.where(c == 0, other, own)

    loads_low, loads_high = by_core(loads_mine, loads_other)
    load_0c = jnp.concatenate([loads_low[:, :32], loads_high[:, :32]], 1)
    load_1c = jnp.concatenate([loads_low[:, 32:96], loads_high[:, 32:96]], 1)
    load_2c = jnp.concatenate([loads_low[:, 96:], loads_high[:, 96:]], 1)
    above = lax.dynamic_slice_in_dim(above_in, z * 8, 8, 1).T

    couple_2 = lax.all_gather(panel_2[1], "z", axis=0, tiled=True)
    couple_2, got = lax.optimization_barrier((couple_2, got))
    couple_2o = lax.ppermute(couple_2, "c", SWAP)
    vec = got.reshape(16, 8, 2, 64).transpose(2, 1, 0, 3).reshape(2, 8, 1024)

    def chip_nt(vector, own, other):
        width = own.shape[1]
        low, high = vector[:, :width], vector[:, width:]
        mine, rest = jnp.where(c == 0, low, high), jnp.where(c == 0, high, low)
        return dot_nt(mine, own) + dot_nt(rest, other)

    u_send = vec[1].reshape(2, 4, 1024)
    u_send = jnp.broadcast_to(u_send[None], (4, 2, 4, 1024)).reshape(8, 4, 1024)
    y_send = vec[0].reshape(2, 4, 4, 256).transpose(2, 1, 0, 3).reshape(4, 4, 512)
    y_send = jnp.concatenate([y_send, y_send], 0)
    got = exchange(jnp.concatenate([u_send, y_send], 2), ("y", "c"))
    got = got.reshape(2, 4, 4, 1536).sum(1)
    update = got[..., :1024]
    y3_piece = lax.dynamic_index_in_dim(got[..., 1024:], y >> 1, 0, keepdims=False)
    y3_piece = jnp.concatenate([y3_piece[:, :256], y3_piece[:, 256:]], 0)

    def lifted(update, base, block, count):
        maps = lax.dynamic_slice_in_dim(block_maps, base, 2, 0).reshape(32)
        targets = block * count + jnp.arange(count, dtype=jnp.int32)
        targets = jnp.concatenate([targets, targets + 16])
        chosen = (maps[:, None] == targets[None, :]).astype(jnp.float32)
        blocks = update.reshape(2, 4, 16, 64).transpose(1, 0, 2, 3).reshape(4, 32, 64)
        placed = jnp.einsum("rnk,np->rpk", blocks, chosen, precision=exact)
        separator = placed[:, :count].reshape(4, count * 64)
        border = placed[:, count:].reshape(4, count * 64)
        whole = jnp.zeros((4, 1024), jnp.float32)
        border = lax.dynamic_update_slice_in_dim(whole, border, block * count * 64, 1)
        return separator, border

    separator, border = lifted(update, 6 + 2 * x, y, 4)
    b_2 = separator + load_2c
    update = border - chip_nt(b_2, couple_2, couple_2o)
    update = exchange(to_all(update, 8), ("xl", "y")).reshape(2, 4, 4, 1024).sum(1)

    gathered, update = lax.optimization_barrier((gathered, update))
    upper = gathered[:, 512:]
    upper_o = lax.ppermute(upper, "c", SWAP)
    pivot_2, pivot_2o = upper[:, :128], upper_o[:, :128]
    panel_1g, panel_1o = upper[:, 128:256], upper_o[:, 128:256]
    panel_0g, panel_0o = upper[:, 256:320], upper_o[:, 256:320]
    separator, border = lifted(update, 2 + 2 * xh, 4 * xl + y, 2)
    b_1 = separator + load_1c
    update = border - chip_nt(b_1, panel_1g[:, 64:], panel_1o[:, 64:])
    update = exchange(to_all(update, 16), ("xh", "xl", "y")).reshape(2, 8, 4, 1024).sum(1)

    separator, border = lifted(update, 0, 4 * x + y, 1)
    b_0 = separator + load_0c
    y0_part = chip_nt(b_0, panel_0g[:, :32], panel_0o[:, :32])
    u0_part = border - chip_nt(b_0, panel_0g[:, 32:], panel_0o[:, 32:])
    y1_part = chip_nt(b_1, panel_1g[:, :64], panel_1o[:, :64])
    y2_part = chip_nt(b_2, pivot_2, pivot_2o)
    u0_send = u0_part.reshape(4, 16, 64).transpose(1, 0, 2)
    y1_send = y1_part.reshape(4, 8, 128).transpose(1, 0, 2)
    y1_send = jnp.concatenate([y1_send, y1_send], 0)
    y2_send = y2_part.reshape(4, 4, 256).transpose(1, 0, 2)
    y2_send = to_all(y2_send, 4).reshape(16, 4, 256)
    payload = jnp.concatenate([to_all(y0_part, 16), y2_send, y1_send, u0_send], 2)
    got = exchange(payload, ("xh", "xl", "y"))
    y_0 = got[..., :1024].sum(0)
    u0_piece = got[..., 1408:].sum(0)
    y1_piece = got[..., 1280:1408].reshape(2, 8, 4, 128).sum(1)
    y1_piece = lax.dynamic_index_in_dim(y1_piece, xh, 0, keepdims=False)
    y2_piece = got[..., 1024:1280].reshape(4, 4, 4, 256).sum(1)
    y2_piece = lax.dynamic_index_in_dim(y2_piece, x, 0, keepdims=False)

    def taken(row, x_vec, s_vec):
        chosen_map = lax.dynamic_index_in_dim(block_maps, row, 0, keepdims=False)
        targets = jnp.arange(32, dtype=jnp.int32)
        chosen = (targets[:, None] == chosen_map[None, :]).astype(jnp.float32)
        stacked = jnp.concatenate([x_vec, s_vec], 1).reshape(8, 32, 64)
        return jnp.einsum("rqk,qn->rnk", stacked, chosen, precision=exact).reshape(8, 1024)

    def paired(y_vec, s_vec, panel):
        both = dot_nn(jnp.concatenate([y_vec, s_vec], 0), panel)
        rows, width = y_vec.shape[0], panel.shape[1] // 2
        return both[:rows, :width] - both[rows:, width:]

    above_mine = jnp.where(c == 0, above[:4], above[4:])
    own = paired(y_0, above_mine, panel_0g)
    other = paired(y_0, above_mine, panel_0o)
    x0_piece = jnp.concatenate(by_core(own, other), 1)
    same = jnp.concatenate([x0_piece, u0_piece, y1_piece], 1)
    got = exchange(to_all(same, 32), LEAF).reshape(16, 2, 4, 256)
    x_0 = got[..., :64].transpose(1, 2, 0, 3).reshape(8, 1024)
    u_0 = got[..., 64:128].transpose(1, 2, 0, 3).reshape(8, 1024)
    y_1 = got[..., 128:].reshape(2, 8, 2, 4, 128)
    y_1 = lax.dynamic_index_in_dim(y_1, xh, 0, keepdims=False)
    y_1 = y_1.transpose(1, 2, 0, 3).reshape(8, 1024)

    s_1 = taken(xh, x_0, above)
    x1_piece = paired(y_1, s_1, panel_1g)
    y2_piece = jnp.concatenate([y2_piece[:, :128], y2_piece[:, 128:]], 0)
    got = exchange(to_all(jnp.concatenate([x1_piece, y2_piece], 1), 16), ("xl", "y", "c"))
    x_1 = got[..., :64].transpose(1, 0, 2).reshape(8, 1024)
    y_2 = lax.dynamic_index_in_dim(
        got[..., 64:].reshape(2, 4, 2, 2, 4, 128), xl, 0, keepdims=False
    )
    y_2 = y_2.transpose(1, 3, 0, 2, 4).reshape(8, 1024)

    s_2 = taken(2 + x, x_1, s_1)
    x2_piece = dot_nn(y_2, pivot_2) - dot_nn(s_2, couple_2)
    got = exchange(to_all(jnp.concatenate([x2_piece, y3_piece], 1), 8), ("y", "c"))
    x_2 = got[..., :128].transpose(1, 0, 2).reshape(8, 1024)
    y_3 = lax.dynamic_index_in_dim(got[..., 128:].reshape(2, 4, 8, 256), y >> 1, 0, keepdims=False)
    y_3 = y_3.transpose(1, 0, 2).reshape(8, 1024)

    s_3 = taken(6 + front_3, x_2, s_2)
    x3_piece = paired(y_3, s_3, gathered[:, :512])

    def to_rows(piece):
        return piece.reshape(8, 16, -1).transpose(1, 0, 2)

    x0_own = lax.dynamic_slice_in_dim(x_0, 64 * (4 * x + y) + 32 * c, 32, 1)
    payload = jnp.concatenate(
        [
            to_rows(x3_piece),
            to_rows(x2_piece),
            to_rows(x1_piece),
            to_rows(x0_own),
            jnp.zeros((16, 8, 34), jnp.float32),
            u_0.reshape(8, 16, 64).transpose(1, 0, 2),
        ],
        2,
    )
    got = exchange(payload, "z")
    return pl.pallas_call(
        last_rows,
        out_shape=[shape(2, 128), shape(4, 128), shape(8, 128), shape(16, 128), shape(64, 128)],
    )(got)


def solution(mesh):
    fine = Mesh(mesh.devices.reshape(2, 2, 4, 2, 16), ("xh", "xl", "y", "c", "z"))
    panel = P(None, "z", LEAF)
    load = P(LEAF, None)
    in_specs = (panel,) * 4 + (load,) * 4 + (P(None, "z", None), P(), P())
    out_specs = (P(LEAF + ("z",), None),) * 4 + (P("z", None),)
    return jax.shard_map(
        on_device, mesh=fine, in_specs=in_specs, out_specs=out_specs, check_vma=False
    )
```

```python
import jax
import jax.numpy as jnp
from jax import lax
from jax.experimental import pallas as pl
from jax.experimental.pallas import tpu as pltpu
from jax.sharding import Mesh, PartitionSpec as P

exact = lax.Precision.HIGHEST
LEAF = ("xh", "xl", "y", "c")
SWAP = [(0, 1), (1, 0)]


def dot_nt(left, right):
    return lax.dot_general(left, right, (((1,), (1,)), ((), ())), precision=exact)


def dot_nn(left, right):
    return lax.dot_general(left, right, (((1,), (0,)), ((), ())), precision=exact)


def exchange(value, axes):
    return lax.all_to_all(value, axes, 0, 0)


def to_all(value, count):
    return jnp.broadcast_to(value[None], (count,) + value.shape)


def shape(*dims):
    return jax.ShapeDtypeStruct(dims, jnp.float32)


def pack_upper(p0_ref, p1_ref, p2_ref, out_ref):
    blank = jnp.zeros((64, 64), jnp.float32)
    out_ref[:, :128] = p2_ref[0]
    out_ref[:, 128:256] = jnp.concatenate([p1_ref[0], p1_ref[1]], 1)
    out_ref[:, 256:] = jnp.concatenate([p0_ref[0].T, p0_ref[1].T, blank], 1)


def pack_lower(p2_ref, p3_ref, upper_ref, out_ref):
    out_ref[:, :256] = p3_ref[0]
    out_ref[:, 256:512] = p3_ref[1]
    out_ref[:, 512:640] = p2_ref[1]
    out_ref[:, 640:] = upper_ref[:, :256]


def first_parts(panel_ref, load_ref, inflow_ref, out_ref):
    x = 2 * lax.axis_index("xh") + lax.axis_index("xl")
    y, c = lax.axis_index("y"), lax.axis_index("c")
    keep = dot_nn(panel_ref[0], load_ref[...])
    take = dot_nn(panel_ref[1], load_ref[...])
    border = inflow_ref[2 * x + (y >> 1)]
    first = jnp.where((y & 1) + c == 0, 1.0, 0.0)
    both = jnp.concatenate([keep, first * border - take], 0)
    out_ref[...] = both.T.reshape(16, 8, 128)


def last_rows(got_ref, *out_refs):
    rows = got_ref[...].reshape(128, 128).T
    for ref, start in zip(out_refs, (28, 24, 16, 0, 64)):
        ref[...] = rows[start : start + ref.shape[0]]


def on_device(
    panel_0,
    panel_1,
    panel_2,
    panel_3,
    load_0,
    load_1,
    load_2,
    load_3,
    inflow,
    above_solution,
    block_maps,
):
    xh, xl = lax.axis_index("xh"), lax.axis_index("xl")
    y, c, z = lax.axis_index("y"), lax.axis_index("c"), lax.axis_index("z")
    x = 2 * xh + xl
    y_low = y & 1
    front_3 = 2 * x + (y >> 1)

    rows = pl.pallas_call(pack_upper, out_shape=shape(64, 384))(
        panel_0.transpose(0, 2, 1), panel_1, panel_2
    )
    upper = lax.all_gather(rows, "z", axis=0, tiled=True)
    rows, panel_3, load_3, inflow = lax.optimization_barrier((rows, panel_3, load_3, inflow))

    payload = pl.pallas_call(first_parts, out_shape=shape(16, 8, 128))(panel_3, load_3, inflow)
    payload, loads, above_in = lax.optimization_barrier(
        (payload, (load_0, load_1, load_2), above_solution)
    )
    got = exchange(payload, "z")

    loads = jnp.concatenate(loads, 0)
    loads = lax.dynamic_slice_in_dim(loads, z * 8, 8, 1).T
    loads_mine, loads_sent = jnp.where(c == 0, loads[:4], loads[4:]), jnp.where(c == 0, loads[4:], loads[:4])
    loads_other = lax.ppermute(loads_sent, "c", SWAP)

    def by_core(own, other):
        return jnp.where(c == 0, own, other), jnp.where(c == 0, other, own)

    loads_low, loads_high = by_core(loads_mine, loads_other)
    load_0c = jnp.concatenate([loads_low[:, :32], loads_high[:, :32]], 1)
    load_1c = jnp.concatenate([loads_low[:, 32:96], loads_high[:, 32:96]], 1)
    load_2c = jnp.concatenate([loads_low[:, 96:], loads_high[:, 96:]], 1)
    above = lax.dynamic_slice_in_dim(above_in, z * 8, 8, 1).T

    couple_2 = lax.all_gather(panel_2[1], "z", axis=0, tiled=True)
    couple_2, got = lax.optimization_barrier((couple_2, got))
    couple_2o = lax.ppermute(couple_2, "c", SWAP)
    lower, _ = lax.optimization_barrier((panel_3, got))
    lower = pl.pallas_call(pack_lower, out_shape=shape(64, 896))(panel_2, lower, rows)
    lower = lax.all_gather(lower, "z", axis=0, tiled=True)
    vec = got.reshape(16, 8, 2, 64).transpose(2, 1, 0, 3).reshape(2, 8, 1024)

    def chip_nt(vector, own, other):
        width = own.shape[1]
        low, high = vector[:, :width], vector[:, width:]
        mine, rest = jnp.where(c == 0, low, high), jnp.where(c == 0, high, low)
        return dot_nt(mine, own) + dot_nt(rest, other)

    u_send = vec[1].reshape(2, 4, 1024)
    u_send = jnp.broadcast_to(u_send[None], (4, 2, 4, 1024)).reshape(8, 4, 1024)
    y_send = vec[0].reshape(2, 4, 4, 256).transpose(2, 1, 0, 3).reshape(4, 4, 512)
    y_send = jnp.concatenate([y_send, y_send], 0)
    got = exchange(jnp.concatenate([u_send, y_send], 2), ("y", "c"))
    got = got.reshape(2, 4, 4, 1536).sum(1)
    update = got[..., :1024]
    y3_piece = lax.dynamic_index_in_dim(got[..., 1024:], y >> 1, 0, keepdims=False)
    y3_piece = jnp.concatenate([y3_piece[:, :256], y3_piece[:, 256:]], 0)

    def lifted(update, base, block, count):
        maps = lax.dynamic_slice_in_dim(block_maps, base, 2, 0).reshape(32)
        targets = block * count + jnp.arange(count, dtype=jnp.int32)
        targets = jnp.concatenate([targets, targets + 16])
        chosen = (maps[:, None] == targets[None, :]).astype(jnp.float32)
        blocks = update.reshape(2, 4, 16, 64).transpose(1, 0, 2, 3).reshape(4, 32, 64)
        placed = jnp.einsum("rnk,np->rpk", blocks, chosen, precision=exact)
        separator = placed[:, :count].reshape(4, count * 64)
        border = placed[:, count:].reshape(4, count * 64)
        whole = jnp.zeros((4, 1024), jnp.float32)
        border = lax.dynamic_update_slice_in_dim(whole, border, block * count * 64, 1)
        return separator, border

    separator, border = lifted(update, 6 + 2 * x, y, 4)
    b_2 = separator + load_2c
    update = border - chip_nt(b_2, couple_2, couple_2o)
    upper, _ = lax.optimization_barrier((upper, update))
    upper_o = lax.ppermute(upper, "c", SWAP)

    def split(value):
        return lax.optimization_barrier((value[:, :128], value[:, 128:256], value[:, 256:320]))

    pivot_2, panel_1g, panel_0g = split(upper)
    pivot_2o, panel_1o, panel_0o = split(upper_o)
    update = exchange(to_all(update, 8), ("xl", "y")).reshape(2, 4, 4, 1024).sum(1)

    separator, border = lifted(update, 2 + 2 * xh, 4 * xl + y, 2)
    b_1 = separator + load_1c
    update = border - chip_nt(b_1, panel_1g[:, 64:], panel_1o[:, 64:])
    update = exchange(to_all(update, 16), ("xh", "xl", "y")).reshape(2, 8, 4, 1024).sum(1)

    separator, border = lifted(update, 0, 4 * x + y, 1)
    b_0 = separator + load_0c
    y0_part = chip_nt(b_0, panel_0g[:, :32], panel_0o[:, :32])
    u0_part = border - chip_nt(b_0, panel_0g[:, 32:], panel_0o[:, 32:])
    y1_part = chip_nt(b_1, panel_1g[:, :64], panel_1o[:, :64])
    y2_part = chip_nt(b_2, pivot_2, pivot_2o)
    u0_send = u0_part.reshape(4, 16, 64).transpose(1, 0, 2)
    y1_send = y1_part.reshape(4, 8, 128).transpose(1, 0, 2)
    y1_send = jnp.concatenate([y1_send, y1_send], 0)
    y2_send = y2_part.reshape(4, 4, 256).transpose(1, 0, 2)
    y2_send = to_all(y2_send, 4).reshape(16, 4, 256)
    payload = jnp.concatenate([to_all(y0_part, 16), y2_send, y1_send, u0_send], 2)
    got = exchange(payload, ("xh", "xl", "y"))
    y_0 = got[..., :1024].sum(0)
    u0_piece = got[..., 1408:].sum(0)
    y1_piece = got[..., 1280:1408].reshape(2, 8, 4, 128).sum(1)
    y1_piece = lax.dynamic_index_in_dim(y1_piece, xh, 0, keepdims=False)
    y2_piece = got[..., 1024:1280].reshape(4, 4, 4, 256).sum(1)
    y2_piece = lax.dynamic_index_in_dim(y2_piece, x, 0, keepdims=False)

    def taken(row, x_vec, s_vec):
        chosen_map = lax.dynamic_index_in_dim(block_maps, row, 0, keepdims=False)
        targets = jnp.arange(32, dtype=jnp.int32)
        chosen = (targets[:, None] == chosen_map[None, :]).astype(jnp.float32)
        stacked = jnp.concatenate([x_vec, s_vec], 1).reshape(8, 32, 64)
        return jnp.einsum("rqk,qn->rnk", stacked, chosen, precision=exact).reshape(8, 1024)

    def paired(y_vec, s_vec, panel):
        both = dot_nn(jnp.concatenate([y_vec, s_vec], 0), panel)
        rows, width = y_vec.shape[0], panel.shape[1] // 2
        return both[:rows, :width] - both[rows:, width:]

    above_mine = jnp.where(c == 0, above[:4], above[4:])
    own = paired(y_0, above_mine, panel_0g)
    other = paired(y_0, above_mine, panel_0o)
    x0_piece = jnp.concatenate(by_core(own, other), 1)
    same = jnp.concatenate([x0_piece, u0_piece, y1_piece], 1)
    got = exchange(to_all(same, 32), LEAF).reshape(16, 2, 4, 256)
    x_0 = got[..., :64].transpose(1, 2, 0, 3).reshape(8, 1024)
    u_0 = got[..., 64:128].transpose(1, 2, 0, 3).reshape(8, 1024)
    y_1 = got[..., 128:].reshape(2, 8, 2, 4, 128)
    y_1 = lax.dynamic_index_in_dim(y_1, xh, 0, keepdims=False)
    y_1 = y_1.transpose(1, 2, 0, 3).reshape(8, 1024)

    s_1 = taken(xh, x_0, above)
    x1_piece = paired(y_1, s_1, panel_1g)
    y2_piece = jnp.concatenate([y2_piece[:, :128], y2_piece[:, 128:]], 0)
    got = exchange(to_all(jnp.concatenate([x1_piece, y2_piece], 1), 16), ("xl", "y", "c"))
    x_1 = got[..., :64].transpose(1, 0, 2).reshape(8, 1024)
    y_2 = lax.dynamic_index_in_dim(
        got[..., 64:].reshape(2, 4, 2, 2, 4, 128), xl, 0, keepdims=False
    )
    y_2 = y_2.transpose(1, 3, 0, 2, 4).reshape(8, 1024)

    s_2 = taken(2 + x, x_1, s_1)
    x2_piece = dot_nn(y_2, pivot_2) - dot_nn(s_2, couple_2)
    got = exchange(to_all(jnp.concatenate([x2_piece, y3_piece], 1), 8), ("y", "c"))
    x_2 = got[..., :128].transpose(1, 0, 2).reshape(8, 1024)
    y_3 = lax.dynamic_index_in_dim(got[..., 128:].reshape(2, 4, 8, 256), y >> 1, 0, keepdims=False)
    y_3 = y_3.transpose(1, 0, 2).reshape(8, 1024)

    s_3 = taken(6 + front_3, x_2, s_2)
    x3_piece = paired(y_3, s_3, lower[:, :512])

    def to_rows(piece):
        return piece.reshape(8, 16, -1).transpose(1, 0, 2)

    x0_own = lax.dynamic_slice_in_dim(x_0, 64 * (4 * x + y) + 32 * c, 32, 1)
    payload = jnp.concatenate(
        [
            to_rows(x3_piece),
            to_rows(x2_piece),
            to_rows(x1_piece),
            to_rows(x0_own),
            jnp.zeros((16, 8, 34), jnp.float32),
            u_0.reshape(8, 16, 64).transpose(1, 0, 2),
        ],
        2,
    )
    got = exchange(payload, "z")
    return pl.pallas_call(
        last_rows,
        out_shape=[shape(2, 128), shape(4, 128), shape(8, 128), shape(16, 128), shape(64, 128)],
    )(got)


def solution(mesh):
    fine = Mesh(mesh.devices.reshape(2, 2, 4, 2, 16), ("xh", "xl", "y", "c", "z"))
    panel = P(None, "z", LEAF)
    load = P(LEAF, None)
    in_specs = (panel,) * 4 + (load,) * 4 + (P(None, "z", None), P(), P())
    out_specs = (P(LEAF + ("z",), None),) * 4 + (P("z", None),)
    return jax.shard_map(
        on_device, mesh=fine, in_specs=in_specs, out_specs=out_specs, check_vma=False
    )
```

```python
import jax
import jax.numpy as jnp
from jax import lax
from jax.experimental import pallas as pl
from jax.experimental.pallas import tpu as pltpu
from jax.sharding import Mesh, PartitionSpec as P

exact = lax.Precision.HIGHEST
LEAF = ("xh", "xl", "y", "c")
SWAP = [(0, 1), (1, 0)]


def dot_nt(left, right):
    return lax.dot_general(left, right, (((1,), (1,)), ((), ())), precision=exact)


def dot_nn(left, right):
    return lax.dot_general(left, right, (((1,), (0,)), ((), ())), precision=exact)


def exchange(value, axes):
    return lax.all_to_all(value, axes, 0, 0)


def to_all(value, count):
    return jnp.broadcast_to(value[None], (count,) + value.shape)


def shape(*dims):
    return jax.ShapeDtypeStruct(dims, jnp.float32)


def pack_upper(p0_ref, p1_ref, p2_ref, out_ref):
    blank = jnp.zeros((64, 64), jnp.float32)
    out_ref[:, :128] = p2_ref[0]
    out_ref[:, 128:256] = jnp.concatenate([p1_ref[0], p1_ref[1]], 1)
    out_ref[:, 256:] = jnp.concatenate([p0_ref[0].T, p0_ref[1].T, blank], 1)


def pack_lower(p2_ref, p3_ref, upper_ref, out_ref):
    out_ref[:, :256] = p3_ref[0]
    out_ref[:, 256:512] = p3_ref[1]
    out_ref[:, 512:640] = p2_ref[1]
    out_ref[:, 640:] = upper_ref[:, :256]


def first_parts(panel_ref, load_ref, inflow_ref, out_ref):
    x = 2 * lax.axis_index("xh") + lax.axis_index("xl")
    y, c = lax.axis_index("y"), lax.axis_index("c")
    keep = dot_nn(panel_ref[0], load_ref[...])
    take = dot_nn(panel_ref[1], load_ref[...])
    border = inflow_ref[2 * x + (y >> 1)]
    first = jnp.where((y & 1) + c == 0, 1.0, 0.0)
    both = jnp.concatenate([keep, first * border - take], 0)
    out_ref[...] = both.T.reshape(16, 8, 128)


def last_rows(got_ref, *out_refs):
    rows = got_ref[...].reshape(128, 128).T
    for ref, start in zip(out_refs, (28, 24, 16, 0, 64)):
        ref[...] = rows[start : start + ref.shape[0]]


def on_device(
    panel_0,
    panel_1,
    panel_2,
    panel_3,
    load_0,
    load_1,
    load_2,
    load_3,
    inflow,
    above_solution,
    block_maps,
):
    xh, xl = lax.axis_index("xh"), lax.axis_index("xl")
    y, c, z = lax.axis_index("y"), lax.axis_index("c"), lax.axis_index("z")
    x = 2 * xh + xl
    y_low = y & 1
    front_3 = 2 * x + (y >> 1)

    rows = pl.pallas_call(pack_upper, out_shape=shape(64, 384))(
        panel_0.transpose(0, 2, 1), panel_1, panel_2
    )
    upper = lax.all_gather(rows, "z", axis=0, tiled=True)
    rows, panel_3, load_3, inflow = lax.optimization_barrier((rows, panel_3, load_3, inflow))

    payload = pl.pallas_call(first_parts, out_shape=shape(16, 8, 128))(panel_3, load_3, inflow)
    payload, lane = lax.optimization_barrier((payload, z * 8))
    got = exchange(payload, "z")

    loads = jnp.concatenate([load_0, load_1, load_2], 0)
    loads = lax.dynamic_slice_in_dim(loads, lane, 8, 1).T
    loads_mine, loads_sent = jnp.where(c == 0, loads[:4], loads[4:]), jnp.where(c == 0, loads[4:], loads[:4])
    loads_other = lax.ppermute(loads_sent, "c", SWAP)

    def by_core(own, other):
        return jnp.where(c == 0, own, other), jnp.where(c == 0, other, own)

    loads_low, loads_high = by_core(loads_mine, loads_other)
    load_0c = jnp.concatenate([loads_low[:, :32], loads_high[:, :32]], 1)
    load_1c = jnp.concatenate([loads_low[:, 32:96], loads_high[:, 32:96]], 1)
    load_2c = jnp.concatenate([loads_low[:, 96:], loads_high[:, 96:]], 1)
    above = lax.dynamic_slice_in_dim(above_solution, lane, 8, 1).T

    couple_2 = lax.all_gather(panel_2[1], "z", axis=0, tiled=True)
    couple_2, got = lax.optimization_barrier((couple_2, got))
    couple_2o = lax.ppermute(couple_2, "c", SWAP)
    lower, _ = lax.optimization_barrier((panel_3, got))
    lower = pl.pallas_call(pack_lower, out_shape=shape(64, 896))(panel_2, lower, rows)
    lower = lax.all_gather(lower, "z", axis=0, tiled=True)
    vec = got.reshape(16, 8, 2, 64).transpose(2, 1, 0, 3).reshape(2, 8, 1024)

    def chip_nt(vector, own, other):
        width = own.shape[1]
        low, high = vector[:, :width], vector[:, width:]
        mine, rest = jnp.where(c == 0, low, high), jnp.where(c == 0, high, low)
        return dot_nt(mine, own) + dot_nt(rest, other)

    u_send = vec[1].reshape(2, 4, 1024)
    u_send = jnp.broadcast_to(u_send[None], (4, 2, 4, 1024)).reshape(8, 4, 1024)
    y_send = vec[0].reshape(2, 4, 4, 256).transpose(2, 1, 0, 3).reshape(4, 4, 512)
    y_send = jnp.concatenate([y_send, y_send], 0)
    got = exchange(jnp.concatenate([u_send, y_send], 2), ("y", "c"))
    got = got.reshape(2, 4, 4, 1536).sum(1)
    update = got[..., :1024]
    y3_piece = lax.dynamic_index_in_dim(got[..., 1024:], y >> 1, 0, keepdims=False)
    y3_piece = jnp.concatenate([y3_piece[:, :256], y3_piece[:, 256:]], 0)

    def lifted(update, base, block, count):
        maps = lax.dynamic_slice_in_dim(block_maps, base, 2, 0).reshape(32)
        targets = block * count + jnp.arange(count, dtype=jnp.int32)
        targets = jnp.concatenate([targets, targets + 16])
        chosen = (maps[:, None] == targets[None, :]).astype(jnp.float32)
        blocks = update.reshape(2, 4, 16, 64).transpose(1, 0, 2, 3).reshape(4, 32, 64)
        placed = jnp.einsum("rnk,np->rpk", blocks, chosen, precision=exact)
        separator = placed[:, :count].reshape(4, count * 64)
        border = placed[:, count:].reshape(4, count * 64)
        whole = jnp.zeros((4, 1024), jnp.float32)
        border = lax.dynamic_update_slice_in_dim(whole, border, block * count * 64, 1)
        return separator, border

    separator, border = lifted(update, 6 + 2 * x, y, 4)
    b_2 = separator + load_2c
    update = border - chip_nt(b_2, couple_2, couple_2o)
    upper, _ = lax.optimization_barrier((upper, update))
    upper_o = lax.ppermute(upper, "c", SWAP)

    def split(value):
        return lax.optimization_barrier((value[:, :128], value[:, 128:256], value[:, 256:320]))

    pivot_2, panel_1g, panel_0g = split(upper)
    pivot_2o, panel_1o, panel_0o = split(upper_o)
    update = exchange(to_all(update, 8), ("xl", "y")).reshape(2, 4, 4, 1024).sum(1)

    separator, border = lifted(update, 2 + 2 * xh, 4 * xl + y, 2)
    b_1 = separator + load_1c
    update = border - chip_nt(b_1, panel_1g[:, 64:], panel_1o[:, 64:])
    update = exchange(to_all(update, 16), ("xh", "xl", "y")).reshape(2, 8, 4, 1024).sum(1)

    separator, border = lifted(update, 0, 4 * x + y, 1)
    b_0 = separator + load_0c
    y0_part = chip_nt(b_0, panel_0g[:, :32], panel_0o[:, :32])
    u0_part = border - chip_nt(b_0, panel_0g[:, 32:], panel_0o[:, 32:])
    y1_part = chip_nt(b_1, panel_1g[:, :64], panel_1o[:, :64])
    y2_part = chip_nt(b_2, pivot_2, pivot_2o)
    u0_send = u0_part.reshape(4, 16, 64).transpose(1, 0, 2)
    y1_send = y1_part.reshape(4, 8, 128).transpose(1, 0, 2)
    y1_send = jnp.concatenate([y1_send, y1_send], 0)
    y2_send = y2_part.reshape(4, 4, 256).transpose(1, 0, 2)
    y2_send = to_all(y2_send, 4).reshape(16, 4, 256)
    payload = jnp.concatenate([to_all(y0_part, 16), y2_send, y1_send, u0_send], 2)
    got = exchange(payload, ("xh", "xl", "y"))
    y_0 = got[..., :1024].sum(0)
    u0_piece = got[..., 1408:].sum(0)
    y1_piece = got[..., 1280:1408].reshape(2, 8, 4, 128).sum(1)
    y1_piece = lax.dynamic_index_in_dim(y1_piece, xh, 0, keepdims=False)
    y2_piece = got[..., 1024:1280].reshape(4, 4, 4, 256).sum(1)
    y2_piece = lax.dynamic_index_in_dim(y2_piece, x, 0, keepdims=False)

    def taken(row, x_vec, s_vec):
        chosen_map = lax.dynamic_index_in_dim(block_maps, row, 0, keepdims=False)
        targets = jnp.arange(32, dtype=jnp.int32)
        chosen = (targets[:, None] == chosen_map[None, :]).astype(jnp.float32)
        stacked = jnp.concatenate([x_vec, s_vec], 1).reshape(8, 32, 64)
        return jnp.einsum("rqk,qn->rnk", stacked, chosen, precision=exact).reshape(8, 1024)

    def paired(y_vec, s_vec, panel):
        both = dot_nn(jnp.concatenate([y_vec, s_vec], 0), panel)
        rows, width = y_vec.shape[0], panel.shape[1] // 2
        return both[:rows, :width] - both[rows:, width:]

    above_mine = jnp.where(c == 0, above[:4], above[4:])
    own = paired(y_0, above_mine, panel_0g)
    other = paired(y_0, above_mine, panel_0o)
    x0_piece = jnp.concatenate(by_core(own, other), 1)
    same = jnp.concatenate([x0_piece, u0_piece, y1_piece], 1)
    got = exchange(to_all(same, 32), LEAF).reshape(16, 2, 4, 256)
    x_0 = got[..., :64].transpose(1, 2, 0, 3).reshape(8, 1024)
    u_0 = got[..., 64:128].transpose(1, 2, 0, 3).reshape(8, 1024)
    y_1 = got[..., 128:].reshape(2, 8, 2, 4, 128)
    y_1 = lax.dynamic_index_in_dim(y_1, xh, 0, keepdims=False)
    y_1 = y_1.transpose(1, 2, 0, 3).reshape(8, 1024)

    s_1 = taken(xh, x_0, above)
    x1_piece = paired(y_1, s_1, panel_1g)
    y2_piece = jnp.concatenate([y2_piece[:, :128], y2_piece[:, 128:]], 0)
    got = exchange(to_all(jnp.concatenate([x1_piece, y2_piece], 1), 16), ("xl", "y", "c"))
    x_1 = got[..., :64].transpose(1, 0, 2).reshape(8, 1024)
    y_2 = lax.dynamic_index_in_dim(
        got[..., 64:].reshape(2, 4, 2, 2, 4, 128), xl, 0, keepdims=False
    )
    y_2 = y_2.transpose(1, 3, 0, 2, 4).reshape(8, 1024)

    s_2 = taken(2 + x, x_1, s_1)
    x2_piece = dot_nn(y_2, pivot_2) - dot_nn(s_2, couple_2)
    got = exchange(to_all(jnp.concatenate([x2_piece, y3_piece], 1), 8), ("y", "c"))
    x_2 = got[..., :128].transpose(1, 0, 2).reshape(8, 1024)
    y_3 = lax.dynamic_index_in_dim(got[..., 128:].reshape(2, 4, 8, 256), y >> 1, 0, keepdims=False)
    y_3 = y_3.transpose(1, 0, 2).reshape(8, 1024)

    s_3 = taken(6 + front_3, x_2, s_2)
    x3_piece = paired(y_3, s_3, lower[:, :512])

    def to_rows(piece):
        return piece.reshape(8, 16, -1).transpose(1, 0, 2)

    x0_own = lax.dynamic_slice_in_dim(x_0, 64 * (4 * x + y) + 32 * c, 32, 1)
    payload = jnp.concatenate(
        [
            to_rows(x3_piece),
            to_rows(x2_piece),
            to_rows(x1_piece),
            to_rows(x0_own),
            jnp.zeros((16, 8, 34), jnp.float32),
            u_0.reshape(8, 16, 64).transpose(1, 0, 2),
        ],
        2,
    )
    got = exchange(payload, "z")
    return pl.pallas_call(
        last_rows,
        out_shape=[shape(2, 128), shape(4, 128), shape(8, 128), shape(16, 128), shape(64, 128)],
    )(got)


def solution(mesh):
    fine = Mesh(mesh.devices.reshape(2, 2, 4, 2, 16), ("xh", "xl", "y", "c", "z"))
    panel = P(None, "z", LEAF)
    load = P(LEAF, None)
    in_specs = (panel,) * 4 + (load,) * 4 + (P(None, "z", None), P(), P())
    out_specs = (P(LEAF + ("z",), None),) * 4 + (P("z", None),)
    return jax.shard_map(
        on_device, mesh=fine, in_specs=in_specs, out_specs=out_specs, check_vma=False
    )
```
